32 devices in a mesh: dp: 8 (over z, core), expert: 4 (over y, x).
Axes of the slice: x: 2, y: 2, z: 4, core: 2. Of those that a mesh axis runs over, the one named last changes fastest.
Arguments:
- tokens: bfloat16 [512, 4096], P('expert', 'dp'), may hold values from -6 to 6
- cotangent: bfloat16 [512, 4096], P('expert', 'dp'), may hold values from -2.25 to 2.25
- routes: int32 [512, 2], P('expert'), may hold values from 0 to 15, all different within a row; in each aligned block of 128 rows (0 to 127, 128 to 255, ...) at most 40 rows name the same one
- gates: float32 [512, 2], P('expert'), may hold values from 0.05 to 1
- expert_weights: bfloat16 [16, 3, 2048, 4096], P('expert', None, 'dp'), may hold values from -0.09375 to 0.09375
Outputs:
- weight_grads: bfloat16 [16, 3, 2048, 4096], P('expert', None, 'dp')
The draws below stay inside these ranges and needn't reach their ends.
Inputs may be any that keep to these rules, and one draw needn't show every extreme that they name: Each row names 2 different experts; within the 128 rows of one index of the expert axis no expert is named by more than 40 routes.
All inputs are finite; a program needn't handle non-finite values.
Results may differ from the reference program's by a relative error of at most 0.0057.
Values may be sent and summed in bfloat16 or wider, within the bound.
A program may use at most 128 MiB of HBM per device.

```python
import math
import jax
import jax.numpy as jnp
import numpy as np
from jax import lax

D = 4096
FH = 2048
E = 16
KG = 2
TOK_DEV = 128
CAP = 40
TOKENS = 512
ROWS_E = 64


def levels(rng, dims, shards, smallest, top_value):
    def one(dim, blocks):
        steps = jax.random.uniform(jax.random.fold_in(jax.random.fold_in(rng, 6), dim), (blocks,), jnp.float32, smallest / len(shards), top_value / len(shards))
        return jnp.repeat(jnp.exp(steps), dims[dim] // blocks).reshape((-1,) + (1,) * (len(dims) - dim - 1))

    loudness = one(*shards[0])
    for cut in shards[1:]:
        loudness = loudness * one(*cut)
    return loudness


def deal_out(stream_key, own, number, rows, count, top, bound, lean):
    ranking = jax.random.permutation(stream_key, count)
    heavy_load, ordinary = portions_of(count, rows * top, bound, lean, True), portions_of(count, rows * top, bound, lean, False)
    places = jnp.arange(count)

    def named(sizes, offset_by):
        used = int((sizes > 0).sum())
        fixed = max(1, used // 4)
        shifted = fixed + (places - fixed + offset_by * (used - fixed)) % max(1, count - fixed)
        return jnp.zeros((count,), jnp.int32).at[ranking[jnp.where(places < fixed, places, shifted)]].set(jnp.asarray(sizes, jnp.int32))

    sizes = jnp.where(number % 4 == 0, named(heavy_load, number // 4), named(ordinary, number - number // 4 - 1))
    mixed = jax.random.permutation(jax.random.fold_in(own, 3), count)
    giver, sink = mixed[0:count // 2 * 2:2], mixed[1:count // 2 * 2:2]
    room = jnp.minimum(sizes[giver] - 1, bound - sizes[sink]) // 2
    room = jnp.where((giver == ranking[0]) | (sink == ranking[0]) | (sizes[sink] == 0), 0, jnp.maximum(room, 0))
    shifted = jax.random.randint(jax.random.fold_in(own, 4), (count // 2,), 0, 1 << 20) % (room + 1)
    sizes = sizes.at[giver].add(-shifted).at[sink].add(shifted)
    members = jnp.searchsorted(jnp.cumsum(sizes), jnp.arange(rows * top), side="right").astype(jnp.int32)
    table = members.reshape(top, rows).T
    table = table[jax.random.permutation(jax.random.fold_in(own, 1), rows)]
    offset_by = jax.random.randint(jax.random.fold_in(own, 2), (rows, 1), 0, top)
    return jnp.take_along_axis(table, (jnp.arange(top)[None, :] + offset_by) % top, axis=1)


def portions_of(amount, total, bound, lean, full):
    loads = [(1 << 20) // math.isqrt(standing ** lean) + 1 for standing in range(1, amount + 1)]
    largest = bound if full else min(bound, max(-(-total // amount), total * loads[0] // sum(loads)))
    least = 1 if total - largest >= amount - 1 else 0
    holding, surplus = [largest] + [least] * (amount - 1), total - largest - least * (amount - 1)
    while surplus > 0:
        movable = [i for i in range(1, amount) if holding[i] < largest] or [i for i in range(1, amount) if holding[i] < bound]
        mass, left = sum([loads[i] for i in movable]), surplus
        for i in movable:
            extra = min(bound - holding[i], max(1, left * loads[i] // mass), surplus)
            holding[i] = holding[i] + extra
            surplus = surplus - extra
    return np.array(holding)


def normal_values(stream_key, shape, width, limit, split=(), kind=jnp.bfloat16):
    entries = width * jax.random.normal(stream_key, shape, jnp.float32)
    if split:
        entries = entries * levels(stream_key, shape, split, -0.22, 0.18)
    return jnp.clip(entries, -limit, limit).astype(kind)


def setup_inputs(seed: int = 0) -> dict:
    streams_of = jax.random.split(jax.random.key(seed), 6)
    tokens = normal_values(streams_of[0], (TOKENS, D), 1.0, 6.0, ((0, 4), (1, 8)))
    cotangent = normal_values(streams_of[1], (TOKENS, D), (3.0 * ROWS_E ** -0.5), 2.25, ((0, 4), (1, 8)))
    routes_keys = jax.random.split(jax.random.fold_in(streams_of[2], 1), TOKENS // TOK_DEV)
    routes_turns = jax.random.permutation(jax.random.fold_in(streams_of[2], 3), TOKENS // TOK_DEV)
    routes = jax.vmap(lambda own, number: deal_out(jax.random.fold_in(streams_of[2], 2), own, number, TOK_DEV, E, KG, CAP, 2))(routes_keys, routes_turns).reshape((TOKENS, KG))
    gates = jnp.clip(jnp.exp(math.log(1.0) - 2.9957323 * jax.random.uniform(streams_of[3], (TOKENS, KG), jnp.float32) ** levels(streams_of[3], (TOKENS, KG), ((0, 4),), -0.2, 0.2)), 0.05, 1.0)
    expert_weights = normal_values(streams_of[4], (E, 3, FH, D), D ** -0.5, 0.09375, ((0, 4), (2, 8)))
    return {"tokens": tokens, "cotangent": cotangent, "routes": routes, "gates": gates, "expert_weights": expert_weights}


def row_terms(input_rows, scaled, weights):
    ins = input_rows.astype(jnp.float32)
    outs = scaled.astype(jnp.float32)
    gate_part = jnp.dot(input_rows, weights[0].T, preferred_element_type=jnp.float32)
    up_part = jnp.dot(input_rows, weights[1].T, preferred_element_type=jnp.float32)
    sigmoid_part = jax.nn.sigmoid(gate_part)
    hidden = (gate_part * sigmoid_part * up_part).astype(jnp.bfloat16)
    back_hidden = jnp.dot(scaled, weights[2].T, preferred_element_type=jnp.float32)
    derivative = sigmoid_part * (1.0 + gate_part * (1.0 - sigmoid_part))
    pre_gate = (back_hidden * up_part * derivative).astype(jnp.bfloat16)
    pre_up = (back_hidden * gate_part * sigmoid_part).astype(jnp.bfloat16)
    gate_grads = jnp.dot(pre_gate.T, input_rows, preferred_element_type=jnp.float32)
    up_grads = jnp.dot(pre_up.T, input_rows, preferred_element_type=jnp.float32)
    down_grads = jnp.dot(hidden.T, scaled, preferred_element_type=jnp.float32)
    return jnp.stack([gate_grads, up_grads, down_grads], axis=0)


def reference(tokens, cotangent, routes, gates, expert_weights):
    block_rows = 128
    expert_total = expert_weights.shape[0]
    per_token = routes.shape[1]
    routed = routes.reshape(-1).astype(jnp.int32)
    route_total = routed.shape[0]
    sorted_order = jnp.argsort(routed, stable=True).astype(jnp.int32)
    picked = routed[sorted_order]
    matches = (routed[:, None] == jnp.arange(expert_total, dtype=jnp.int32)[None, :]).astype(jnp.int32)
    counts = jnp.sum(matches, axis=0)
    starts = jnp.cumsum(counts) - counts
    padded = (counts + block_rows - 1) // block_rows * block_rows
    limits = jnp.cumsum(padded)
    block_starts = limits - padded
    position = jnp.arange(route_total, dtype=jnp.int32) - starts[picked]
    destination = block_starts[picked] + position
    slot_total = ((route_total + block_rows - 1) // block_rows + expert_total) * block_rows
    source = jnp.full((slot_total,), route_total, jnp.int32).at[destination].set(sorted_order)
    blocks = slot_total // block_rows
    block_first = jnp.arange(blocks, dtype=jnp.int32) * block_rows
    block_expert = jnp.minimum(jnp.sum((limits[None, :] <= block_first[:, None]).astype(jnp.int32), axis=1), expert_total - 1)
    gates_flat = gates.reshape(-1)

    def one_block(running_sum, item):
        index_rows, expert = item
        filled = index_rows < route_total
        clamped = jnp.minimum(index_rows, route_total - 1)
        token_index = clamped // per_token
        input_rows = jnp.where(filled[:, None], tokens[token_index], jnp.zeros((), tokens.dtype))
        weight = jnp.where(filled, gates_flat[clamped], jnp.zeros((), gates_flat.dtype))
        scaled = (weight[:, None] * cotangent[token_index].astype(jnp.float32)).astype(jnp.bfloat16)
        block_term = row_terms(input_rows, scaled, expert_weights[expert])
        return running_sum.at[expert].add(block_term), None

    start_sum = jnp.zeros(expert_weights.shape, jnp.float32)
    final_sum, unused = lax.scan(one_block, start_sum, (source.reshape(blocks, block_rows), block_expert))
    return final_sum.astype(jnp.bfloat16)
```

```python
import functools

import jax
import jax.numpy as jnp
from jax import lax
from jax.experimental import pallas as pl
from jax.experimental.pallas import tpu as pltpu
from jax.sharding import PartitionSpec as P

CAP = 40
CORES = 2
MESH = pl.DeviceIdType.MESH


def exchange_kernel(
    sizes, tok_ref, cot_ref, meta_ref, w_ref,
    rows_ref, pre_ref,
    buf, metab, wbuf, sel, gsel, rows, acc,
    rsem, zsem, esem, bsem, msem_r, msem_s, osem, wsem, rowsem,
):
    chips, groups, local, per_token, length = sizes
    stages = groups.bit_length() - 1
    dp = lax.axis_index("dp")
    own = lax.axis_index("expert")
    z, core = dp // CORES, dp % CORES
    other = 1 - core
    tokens_each, features = tok_ref.shape

    def peer(z_to, core_to, group_to):
        return (z_to * CORES + core_to, group_to)

    def across(index, bit):
        return index + bit - 2 * bit * ((index // bit) % 2)

    def mirror(mask):
        result = own
        for place in range(stages):
            if mask >> place & 1:
                result = across(result, 1 << place)
        return result

    own_copies = [
        pltpu.make_async_copy(ref, buf.at[core, a, z, own], osem.at[a])
        for a, ref in enumerate((tok_ref, cot_ref))
    ] + [pltpu.make_async_copy(meta_ref, metab.at[own], osem.at[2])]
    for copy in own_copies:
        copy.start()

    greeted = [
        peer(lax.rem(z + 1, chips), core, own),
        peer(lax.rem(z + chips - 1, chips), core, own),
        peer(z, other, own),
    ] + [peer(z, core, mirror(mask)) for mask in range(1, groups)]
    barrier = pltpu.get_barrier_semaphore()
    for device in greeted:
        pl.semaphore_signal(barrier, inc=1, device_id=device, device_id_type=MESH)
    pl.semaphore_wait(barrier, len(greeted))
    for copy in own_copies:
        copy.wait()

    def send(c, a, zz, s, sem, device):
        return pltpu.make_async_remote_copy(
            src_ref=buf.at[c, a, zz, s], dst_ref=buf.at[c, a, zz, s],
            send_sem=sem, recv_sem=rsem.at[c, a, zz, s],
            device_id=device, device_id_type=MESH,
        )

    def arrived(c, a, zz, s):
        pltpu.make_async_copy(
            buf.at[c, a, zz, s], buf.at[c, a, zz, s], rsem.at[c, a, zz, s]
        ).wait()

    def to_sibling(a, zz, s):
        send(core, a, zz, s, bsem, peer(z, other, own)).start()

    def bit_of(a, stage):
        return 1 << ((stage + a) % stages)

    def mask_list(a, stage):
        masks = [0]
        for earlier in range(stage):
            masks = masks + [mask ^ bit_of(a, earlier) for mask in masks]
        return masks

    def fresh_masks(a, stage):
        return [mask ^ bit_of(a, stage) for mask in mask_list(a, stage)]

    def nearest(k):
        m = jnp.where(2 * z < chips, z, chips - 1 - z)
        side = jnp.where(k % 2 == 1, z - (k + 1) // 2, z + k // 2)
        rest = jnp.where(2 * z < chips, k, chips - 1 - k)
        return jnp.where(k <= 2 * m, side, rest)

    def z_send(zz, a, upward):
        return send(
            core, a, zz, own, zsem.at[a, zz, 0 if upward else 1],
            peer(z + 1 if upward else z - 1, core, own),
        )

    def z_forward(zz, first):
        for a in range(2):
            if not first:
                arrived(core, a, zz, own)

            @pl.when((zz <= z) & (z < chips - 1))
            def _():
                z_send(zz, a, True).start()

            @pl.when((zz >= z) & (z > 0))
            def _():
                z_send(zz, a, False).start()

            to_sibling(a, zz, own)

    def stage_send(k, stage):
        zz = nearest(k)
        for a in range(2):
            if stage > 0:
                for mask in fresh_masks(a, stage - 1):
                    arrived(core, a, zz, mirror(mask))
            for mask in mask_list(a, stage):
                send(
                    core, a, zz, mirror(mask), esem, peer(z, core, mirror(bit_of(a, stage)))
                ).start()
            if stage > 0:
                for mask in fresh_masks(a, stage - 1):
                    to_sibling(a, zz, mirror(mask))

    def last_arrivals(k):
        zz = nearest(k)
        for a in range(2):
            for mask in fresh_masks(a, stages - 1):
                arrived(core, a, zz, mirror(mask))
                to_sibling(a, zz, mirror(mask))

    contract_last = (((1,), (1,)), ((), ()))

    def compute(k):
        zz = nearest(k)
        for turn in range(2):
            c = core if turn == 0 else other
            if turn == 1:
                for a in range(2):
                    for mask in range(groups):
                        arrived(c, a, zz, mirror(mask))
            f = zz * CORES + c
            columns = pl.ds(pl.multiple_of(f * features, features), features)
            x = buf[c, 0, zz].reshape(groups * tokens_each, features)
            y = buf[c, 1, zz].reshape(groups * tokens_each, features)
            for e in range(local):
                chosen = jnp.dot(
                    sel[e], x, preferred_element_type=jnp.float32
                ).astype(jnp.bfloat16)
                scaled = (
                    jnp.dot(sel[e], y, preferred_element_type=jnp.float32) * gsel[e][:, :1]
                ).astype(jnp.bfloat16)
                rows[f, 0, e] = chosen
                rows[f, 1, e] = scaled
                for part, right in enumerate((chosen, chosen, scaled)):
                    acc[e, part] += lax.dot_general(
                        wbuf[e, part, :, columns], right, contract_last,
                        preferred_element_type=jnp.float32,
                    )
            pltpu.make_async_copy(rows.at[f], rows_ref.at[f], rowsem).start()

    for mask in range(1, groups):
        pltpu.make_async_remote_copy(
            src_ref=metab.at[own], dst_ref=metab.at[own], send_sem=msem_s,
            recv_sem=msem_r.at[own], device_id=peer(z, core, mirror(mask)),
            device_id_type=MESH,
        ).start()
    stage_send(0, 0)
    z_forward(z, True)
    for e in range(local):
        pltpu.make_async_copy(w_ref.at[e], wbuf.at[e], wsem).start()

    acc[...] = jnp.zeros_like(acc)
    for mask in range(1, groups):
        s = mirror(mask)
        pltpu.make_async_copy(metab.at[s], metab.at[s], msem_r.at[s]).wait()
    triangle = (
        lax.broadcasted_iota(jnp.int32, (tokens_each, tokens_each), 0)
        < lax.broadcasted_iota(jnp.int32, (tokens_each, tokens_each), 1)
    ).astype(jnp.bfloat16)
    slots = lax.broadcasted_iota(jnp.int32, (length, tokens_each), 0).astype(jnp.float32)
    for e in range(local):
        wanted = (own * local + e).astype(jnp.float32)
        opening = jnp.zeros((1, 1), jnp.float32)
        gate_sum = jnp.zeros((length, 1), jnp.float32)
        for s in range(groups):
            table = metab[s]
            hit = jnp.zeros((1, tokens_each), jnp.float32)
            gate = jnp.zeros((1, tokens_each), jnp.float32)
            for k in range(per_token):
                same = table[k:k + 1] == wanted
                hit = jnp.where(same, 1.0, hit)
                gate = jnp.where(same, table[per_token + k:per_token + k + 1], gate)
            wide = jnp.broadcast_to(hit, (16, tokens_each)).astype(jnp.bfloat16)
            place = jnp.dot(wide, triangle, preferred_element_type=jnp.float32)[:1] + opening
            opening = opening + jnp.sum(hit, axis=1, keepdims=True)
            picked = (slots == place) & (hit > 0.5)
            sel[e, :, s * tokens_each:(s + 1) * tokens_each] = jnp.where(
                picked, 1.0, 0.0
            ).astype(jnp.bfloat16)
            gate_sum = gate_sum + jnp.sum(
                jnp.where(picked, gate, 0.0), axis=1, keepdims=True
            )
        gsel[e] = jnp.broadcast_to(gate_sum, gsel.shape[1:])

    def step(k, carry):
        @pl.when((k > 0) & (k < chips))
        def _():
            @pl.when(z - k >= 0)
            def _():
                z_forward(z - k, False)

            @pl.when(z + k < chips)
            def _():
                z_forward(z + k, False)

            stage_send(k, 0)

        for stage in range(1, stages):
            @pl.when((k >= stage) & (k < chips + stage))
            def _(stage=stage):
                stage_send(k - stage, stage)

        @pl.when((k >= stages) & (k < chips + stages))
        def _():
            last_arrivals(k - stages)

        @pl.when(k == stages + 1)
        def _():
            pltpu.make_async_copy(w_ref, wbuf, wsem).wait()

        @pl.when(k >= stages + 1)
        def _():
            compute(k - stages - 1)

        return carry

    lax.fori_loop(0, chips + stages + 1, step, 0)

    for e in range(local):
        gate_part, up_part, back = acc[e, 0], acc[e, 1], acc[e, 2]
        sigmoid = jax.nn.sigmoid(gate_part)
        silu = gate_part * sigmoid
        pre_ref[e, 0] = (
            back * up_part * (sigmoid * (1.0 + gate_part * (1.0 - sigmoid)))
        ).astype(jnp.bfloat16)
        pre_ref[e, 1] = (back * silu).astype(jnp.bfloat16)
        pre_ref[e, 2] = (silu * up_part).astype(jnp.bfloat16)

    def z_drain(zz, carry):
        for a in range(2):
            @pl.when((zz <= z) & (z < chips - 1))
            def _():
                z_send(zz, a, True).wait_send()

            @pl.when((zz >= z) & (z > 0))
            def _():
                z_send(zz, a, False).wait_send()

        return carry

    lax.fori_loop(0, chips, z_drain, 0)
    sent = buf.at[0, :, :, pl.ds(0, groups - 1)]
    pltpu.make_async_copy(sent, sent, esem).wait()
    pltpu.make_async_copy(buf.at[0], buf.at[0], bsem).wait()
    sent = metab.at[pl.ds(0, groups - 1)]
    pltpu.make_async_copy(sent, sent, msem_s).wait()
    pltpu.make_async_copy(rows, rows_ref, rowsem).wait()


def outer_kernel(pre_ref, rows_ref, out_ref):
    pieces, features = rows_ref.shape[0], rows_ref.shape[-1]
    for piece in range(pieces):
        columns = slice(piece * features, (piece + 1) * features)
        for part, which in enumerate((0, 0, 1)):
            out_ref[0, part, :, columns] = jnp.dot(
                pre_ref[0, part], rows_ref[piece, which, 0],
                preferred_element_type=jnp.float32,
            ).astype(jnp.bfloat16)


def per_device(tokens, cotangent, routes, gates, expert_weights):
    local, parts, hidden, total_features = expert_weights.shape
    tokens_each, features = tokens.shape
    per_token = routes.shape[1]
    groups = lax.axis_size("expert")
    devices = lax.axis_size("dp")
    chips = devices // CORES
    length = groups * CAP
    meta = jnp.concatenate([routes.astype(jnp.float32), gates], axis=1).T
    meta_rows = -(-meta.shape[0] // 8) * 8
    meta = jnp.pad(meta, ((0, meta_rows - meta.shape[0]), (0, 0)))
    sizes = (chips, groups, local, per_token, length)
    any_space = pl.BlockSpec(memory_space=pl.ANY)
    rows, pre = pl.pallas_call(
        functools.partial(exchange_kernel, sizes),
        out_shape=(
            jax.ShapeDtypeStruct((devices, 2, local, length, features), jnp.bfloat16),
            jax.ShapeDtypeStruct((local, parts, hidden, length), jnp.bfloat16),
        ),
        in_specs=[any_space] * 4,
        out_specs=(any_space, pl.BlockSpec(memory_space=pltpu.VMEM)),
        scratch_shapes=[
            pltpu.VMEM((CORES, 2, chips, groups, tokens_each, features), jnp.bfloat16),
            pltpu.VMEM((groups, meta_rows, tokens_each), jnp.float32),
            pltpu.VMEM(expert_weights.shape, jnp.bfloat16),
            pltpu.VMEM((local, length, groups * tokens_each), jnp.bfloat16),
            pltpu.VMEM((local, length, 128), jnp.float32),
            pltpu.VMEM((devices, 2, local, length, features), jnp.bfloat16),
            pltpu.VMEM((local, parts, hidden, length), jnp.float32),
            pltpu.SemaphoreType.DMA((CORES, 2, chips, groups)),
            pltpu.SemaphoreType.DMA((2, chips, 2)),
            pltpu.SemaphoreType.DMA,
            pltpu.SemaphoreType.DMA,
            pltpu.SemaphoreType.DMA((groups,)),
            pltpu.SemaphoreType.DMA,
            pltpu.SemaphoreType.DMA((3,)),
            pltpu.SemaphoreType.DMA,
            pltpu.SemaphoreType.DMA,
        ],
        compiler_params=pltpu.CompilerParams(
            collective_id=0, has_side_effects=True, vmem_limit_bytes=60 * 1024 * 1024
        ),
        name="exchange",
    )(tokens, cotangent, meta, expert_weights)
    pieces = max(1, devices // 4)
    return pl.pallas_call(
        outer_kernel,
        out_shape=jax.ShapeDtypeStruct(expert_weights.shape, jnp.bfloat16),
        grid=(local, devices // pieces),
        in_specs=[
            pl.BlockSpec((1, parts, hidden, length), lambda e, j: (e, 0, 0, 0)),
            pl.BlockSpec((pieces, 2, 1, length, features), lambda e, j: (j, 0, e, 0, 0)),
        ],
        out_specs=pl.BlockSpec(
            (1, parts, hidden, pieces * features), lambda e, j: (e, 0, 0, j)
        ),
        compiler_params=pltpu.CompilerParams(vmem_limit_bytes=48 * 1024 * 1024),
        name="outer",
    )(pre, rows)


def solution(mesh):
    return jax.shard_map(
        per_device,
        mesh=mesh,
        in_specs=(
            P("expert", "dp"),
            P("expert", "dp"),
            P("expert", None),
            P("expert", None),
            P("expert", None, "dp", None),
        ),
        out_specs=P("expert", None, "dp", None),
        check_vma=False,
    )
```

```python
import functools

import jax
import jax.numpy as jnp
from jax import lax
from jax.experimental import pallas as pl
from jax.experimental.pallas import tpu as pltpu
from jax.sharding import PartitionSpec as P

CAP = 40
CORES = 2
MESH = pl.DeviceIdType.MESH


def exchange_kernel(
    sizes, tok_ref, cot_ref, routes_ref, gates_ref, w_ref,
    rows_ref, pre_ref,
    buf, metab, wbuf, sel, gsel, rows, acc,
    rsem, zsem, esem, bsem, msem_r, msem_s, osem, wsem, rowsem,
):
    chips, groups, local, per_token, length = sizes
    stages = groups.bit_length() - 1
    dp = lax.axis_index("dp")
    own = lax.axis_index("expert")
    z, core = dp // CORES, dp % CORES
    other = 1 - core
    tokens_each, features = tok_ref.shape
    hidden = w_ref.shape[2]

    def peer(z_to, core_to, group_to):
        return (z_to * CORES + core_to, group_to)

    def across(index, bit):
        return index + bit - 2 * bit * ((index // bit) % 2)

    def mirror(mask):
        result = own
        for place in range(stages):
            if mask >> place & 1:
                result = across(result, 1 << place)
        return result

    own_copies = [
        pltpu.make_async_copy(ref, buf.at[core, a, z, own], osem.at[a])
        for a, ref in enumerate((tok_ref, cot_ref))
    ]
    for copy in own_copies:
        copy.start()
    metab[own] = jnp.zeros(metab.shape[1:], jnp.float32)
    metab[own, 0:per_token] = routes_ref[...].astype(jnp.float32)
    metab[own, per_token:2 * per_token] = gates_ref[...]

    greeted = [
        peer(lax.rem(z + 1, chips), core, own),
        peer(lax.rem(z + chips - 1, chips), core, own),
        peer(z, other, own),
    ] + [peer(z, core, mirror(mask)) for mask in range(1, groups)]
    barrier = pltpu.get_barrier_semaphore()
    for device in greeted:
        pl.semaphore_signal(barrier, inc=1, device_id=device, device_id_type=MESH)
    pl.semaphore_wait(barrier, len(greeted))
    for copy in own_copies:
        copy.wait()

    def send(c, a, zz, s, sem, device):
        return pltpu.make_async_remote_copy(
            src_ref=buf.at[c, a, zz, s], dst_ref=buf.at[c, a, zz, s],
            send_sem=sem, recv_sem=rsem.at[c, a, zz, s],
            device_id=device, device_id_type=MESH,
        )

    def arrived(c, a, zz, s):
        pltpu.make_async_copy(
            buf.at[c, a, zz, s], buf.at[c, a, zz, s], rsem.at[c, a, zz, s]
        ).wait()

    def to_sibling(a, zz, s):
        send(core, a, zz, s, bsem, peer(z, other, own)).start()

    def bit_of(a, stage):
        return 1 << ((stage + a) % stages)

    def mask_list(a, stage):
        masks = [0]
        for earlier in range(stage):
            masks = masks + [mask ^ bit_of(a, earlier) for mask in masks]
        return masks

    def fresh_masks(a, stage):
        return [mask ^ bit_of(a, stage) for mask in mask_list(a, stage)]

    def nearest(k):
        m = jnp.where(2 * z < chips, z, chips - 1 - z)
        side = jnp.where(k % 2 == 1, z - (k + 1) // 2, z + k // 2)
        rest = jnp.where(2 * z < chips, k, chips - 1 - k)
        return jnp.where(k <= 2 * m, side, rest)

    def z_send(zz, a, upward):
        return send(
            core, a, zz, own, zsem.at[a, zz, 0 if upward else 1],
            peer(z + 1 if upward else z - 1, core, own),
        )

    def z_forward(zz, first):
        for a in range(2):
            if not first:
                arrived(core, a, zz, own)

            @pl.when((zz <= z) & (z < chips - 1))
            def _():
                z_send(zz, a, True).start()

            @pl.when((zz >= z) & (z > 0))
            def _():
                z_send(zz, a, False).start()

            to_sibling(a, zz, own)

    def stage_send(k, stage):
        zz = nearest(k)
        for a in range(2):
            if stage > 0:
                for mask in fresh_masks(a, stage - 1):
                    arrived(core, a, zz, mirror(mask))
            for mask in mask_list(a, stage):
                send(
                    core, a, zz, mirror(mask), esem, peer(z, core, mirror(bit_of(a, stage)))
                ).start()
            if stage > 0:
                for mask in fresh_masks(a, stage - 1):
                    to_sibling(a, zz, mirror(mask))

    def last_arrivals(k):
        zz = nearest(k)
        for a in range(2):
            for mask in fresh_masks(a, stages - 1):
                arrived(core, a, zz, mirror(mask))
                to_sibling(a, zz, mirror(mask))

    contract_last = (((1,), (1,)), ((), ()))

    def compute(k):
        zz = nearest(k)
        for turn in range(2):
            c = core if turn == 0 else other
            if turn == 1:
                for a in range(2):
                    for mask in range(groups):
                        arrived(c, a, zz, mirror(mask))
            f = zz * CORES + c
            columns = pl.ds(pl.multiple_of(f * features, features), features)
            x = buf[c, 0, zz].reshape(groups * tokens_each, features)
            y = buf[c, 1, zz].reshape(groups * tokens_each, features)
            pick = sel[...].reshape(local * length, groups * tokens_each)
            rows[f, 0] = (
                jnp.dot(pick, x, preferred_element_type=jnp.float32)
                .astype(jnp.bfloat16).reshape(local, length, features)
            )
            rows[f, 1] = (
                (jnp.dot(pick, y, preferred_element_type=jnp.float32) * gsel[:, :1])
                .astype(jnp.bfloat16).reshape(local, length, features)
            )
            for e in range(local):
                acc[e, 0:2] += lax.dot_general(
                    wbuf[e, 0:2, :, columns].reshape(2 * hidden, features), rows[f, 0, e],
                    contract_last, preferred_element_type=jnp.float32,
                ).reshape(2, hidden, length)
                acc[e, 2] += lax.dot_general(
                    wbuf[e, 2, :, columns], rows[f, 1, e],
                    contract_last, preferred_element_type=jnp.float32,
                )
            pltpu.make_async_copy(rows.at[f], rows_ref.at[f], rowsem).start()

    for mask in range(1, groups):
        pltpu.make_async_remote_copy(
            src_ref=metab.at[own], dst_ref=metab.at[own], send_sem=msem_s,
            recv_sem=msem_r.at[own], device_id=peer(z, core, mirror(mask)),
            device_id_type=MESH,
        ).start()
    stage_send(0, 0)
    z_forward(z, True)
    for e in range(local):
        pltpu.make_async_copy(w_ref.at[e], wbuf.at[e], wsem).start()

    acc[...] = jnp.zeros_like(acc)
    for mask in range(1, groups):
        s = mirror(mask)
        pltpu.make_async_copy(metab.at[s], metab.at[s], msem_r.at[s]).wait()
    triangle = (
        lax.broadcasted_iota(jnp.int32, (tokens_each, tokens_each), 0)
        < lax.broadcasted_iota(jnp.int32, (tokens_each, tokens_each), 1)
    ).astype(jnp.bfloat16)
    slots = lax.broadcasted_iota(jnp.int32, (length, tokens_each), 0).astype(jnp.float32)
    for e in range(local):
        wanted = (own * local + e).astype(jnp.float32)
        opening = jnp.zeros((1, 1), jnp.float32)
        gate_sum = jnp.zeros((length, 1), jnp.float32)
        for s in range(groups):
            table = metab[s]
            hit = jnp.zeros((1, tokens_each), jnp.float32)
            gate = jnp.zeros((1, tokens_each), jnp.float32)
            for k in range(per_token):
                same = table[k:k + 1] == wanted
                hit = jnp.where(same, 1.0, hit)
                gate = jnp.where(same, table[per_token + k:per_token + k + 1], gate)
            wide = jnp.broadcast_to(hit, (16, tokens_each)).astype(jnp.bfloat16)
            place = jnp.dot(wide, triangle, preferred_element_type=jnp.float32)[:1] + opening
            opening = opening + jnp.sum(hit, axis=1, keepdims=True)
            picked = (slots == place) & (hit > 0.5)
            sel[e, :, s * tokens_each:(s + 1) * tokens_each] = jnp.where(
                picked, 1.0, 0.0
            ).astype(jnp.bfloat16)
            gate_sum = gate_sum + jnp.sum(
                jnp.where(picked, gate, 0.0), axis=1, keepdims=True
            )
        gsel[e * length:(e + 1) * length] = jnp.broadcast_to(gate_sum, (length, 128))

    def step(k, carry):
        @pl.when((k > 0) & (k < chips))
        def _():
            @pl.when(z - k >= 0)
            def _():
                z_forward(z - k, False)

            @pl.when(z + k < chips)
            def _():
                z_forward(z + k, False)

            stage_send(k, 0)

        for stage in range(1, stages):
            @pl.when((k >= stage) & (k < chips + stage))
            def _(stage=stage):
                stage_send(k - stage, stage)

        @pl.when(k == stages + 1)
        def _():
            pltpu.make_async_copy(w_ref, wbuf, wsem).wait()

        @pl.when(k >= stages + 1)
        def _():
            compute(k - stages - 1)

        @pl.when((k >= stages) & (k < chips + stages))
        def _():
            last_arrivals(k - stages)

        return carry

    lax.fori_loop(0, chips + stages + 1, step, 0)

    if pre_ref.shape[-1] > length:
        pre_ref[:, :, :, length:] = jnp.zeros(
            pre_ref.shape[:3] + (pre_ref.shape[-1] - length,), jnp.bfloat16
        )
    for e in range(local):
        gate_part, up_part, back = acc[e, 0], acc[e, 1], acc[e, 2]
        sigmoid = jax.nn.sigmoid(gate_part)
        silu = gate_part * sigmoid
        pre_ref[e, 0, :, :length] = (
            back * up_part * (sigmoid * (1.0 + gate_part * (1.0 - sigmoid)))
        ).astype(jnp.bfloat16)
        pre_ref[e, 1, :, :length] = (back * silu).astype(jnp.bfloat16)
        pre_ref[e, 2, :, :length] = (silu * up_part).astype(jnp.bfloat16)

    def z_drain(zz, carry):
        for a in range(2):
            @pl.when((zz <= z) & (z < chips - 1))
            def _():
                z_send(zz, a, True).wait_send()

            @pl.when((zz >= z) & (z > 0))
            def _():
                z_send(zz, a, False).wait_send()

        return carry

    lax.fori_loop(0, chips, z_drain, 0)
    sent = buf.at[0, :, :, pl.ds(0, groups - 1)]
    pltpu.make_async_copy(sent, sent, esem).wait()
    pltpu.make_async_copy(buf.at[0], buf.at[0], bsem).wait()
    sent = metab.at[pl.ds(0, groups - 1)]
    pltpu.make_async_copy(sent, sent, msem_s).wait()
    pltpu.make_async_copy(rows, rows_ref, rowsem).wait()


def outer_kernel(
    pieces, length, pre_hbm, rows_ref, out_ref, pre, rbuf, obuf, insem, osem, psem
):
    local, parts, hidden, padded = pre.shape
    devices, features = rbuf.shape[1], rbuf.shape[-1]
    per_expert = devices // pieces
    slots = obuf.shape[0]
    steps = local * per_expert

    def rows_in(e):
        return pltpu.make_async_copy(
            rows_ref.at[:, :, e], rbuf.at[e, :, :, pl.ds(0, length)], insem.at[e]
        )

    def write(step):
        slot = step % slots
        e, j = step // per_expert, step % per_expert
        width = pieces * features
        return pltpu.make_async_copy(
            obuf.at[slot],
            out_ref.at[e, :, :, pl.ds(pl.multiple_of(j * width, width), width)],
            osem.at[slot],
        )

    pre_in = pltpu.make_async_copy(pre_hbm, pre, psem)
    pre_in.start()
    for e in range(local):
        rows_in(e).start()
    if padded > length:
        rbuf[:, :, :, length:] = jnp.zeros(
            rbuf.shape[:3] + (padded - length, features), jnp.bfloat16
        )
    pre_in.wait()

    def one(step, carry):
        slot = step % slots
        e, j = step // per_expert, step % per_expert

        @pl.when(j == 0)
        def _():
            rows_in(e).wait()

        @pl.when(step >= slots)
        def _():
            write(step - slots).wait()

        for piece in range(pieces):
            f = j * pieces + piece
            columns = slice(piece * features, (piece + 1) * features)
            obuf[slot, 0:2, :, columns] = jnp.dot(
                pre[e, 0:2].reshape(2 * hidden, padded), rbuf[e, f, 0],
                preferred_element_type=jnp.float32,
            ).astype(jnp.bfloat16).reshape(2, hidden, features)
            obuf[slot, 2, :, columns] = jnp.dot(
                pre[e, 2], rbuf[e, f, 1], preferred_element_type=jnp.float32
            ).astype(jnp.bfloat16)
        write(step).start()
        return carry

    lax.fori_loop(0, steps, one, 0)
    for step in range(max(0, steps - slots), steps):
        write(step).wait()


def per_device(tokens, cotangent, routes, gates, expert_weights):
    local, parts, hidden, total_features = expert_weights.shape
    tokens_each, features = tokens.shape
    per_token = routes.shape[1]
    groups = lax.axis_size("expert")
    devices = lax.axis_size("dp")
    chips = devices // CORES
    length = groups * CAP
    meta_rows = -(-2 * per_token // 8) * 8
    padded = -(-length // 128) * 128
    sizes = (chips, groups, local, per_token, length)
    any_space = pl.BlockSpec(memory_space=pl.ANY)
    in_vmem = pl.BlockSpec(memory_space=pltpu.VMEM)
    rows, pre = pl.pallas_call(
        functools.partial(exchange_kernel, sizes),
        out_shape=(
            jax.ShapeDtypeStruct((devices, 2, local, length, features), jnp.bfloat16),
            jax.ShapeDtypeStruct((local, parts, hidden, padded), jnp.bfloat16),
        ),
        in_specs=[any_space, any_space, in_vmem, in_vmem, any_space],
        out_specs=(any_space, in_vmem),
        scratch_shapes=[
            pltpu.VMEM((CORES, 2, chips, groups, tokens_each, features), jnp.bfloat16),
            pltpu.VMEM((groups, meta_rows, tokens_each), jnp.float32),
            pltpu.VMEM(expert_weights.shape, jnp.bfloat16),
            pltpu.VMEM((local, length, groups * tokens_each), jnp.bfloat16),
            pltpu.VMEM((local * length, 128), jnp.float32),
            pltpu.VMEM((devices, 2, local, length, features), jnp.bfloat16),
            pltpu.VMEM((local, parts, hidden, length), jnp.float32),
            pltpu.SemaphoreType.DMA((CORES, 2, chips, groups)),
            pltpu.SemaphoreType.DMA((2, chips, 2)),
            pltpu.SemaphoreType.DMA,
            pltpu.SemaphoreType.DMA,
            pltpu.SemaphoreType.DMA((groups,)),
            pltpu.SemaphoreType.DMA,
            pltpu.SemaphoreType.DMA((2,)),
            pltpu.SemaphoreType.DMA,
            pltpu.SemaphoreType.DMA,
        ],
        compiler_params=pltpu.CompilerParams(
            collective_id=0, has_side_effects=True, vmem_limit_bytes=60 * 1024 * 1024
        ),
        name="exchange",
    )(tokens, cotangent, routes.T, gates.T, expert_weights)
    pieces = max(1, devices // 4)
    slots = 5
    return pl.pallas_call(
        functools.partial(outer_kernel, pieces, length),
        out_shape=jax.ShapeDtypeStruct(expert_weights.shape, jnp.bfloat16),
        in_specs=[any_space] * 2,
        out_specs=any_space,
        scratch_shapes=[
            pltpu.VMEM((local, parts, hidden, padded), jnp.bfloat16),
            pltpu.VMEM((local, devices, 2, padded, features), jnp.bfloat16),
            pltpu.VMEM((slots, parts, hidden, pieces * features), jnp.bfloat16),
            pltpu.SemaphoreType.DMA((local,)),
            pltpu.SemaphoreType.DMA((slots,)),
            pltpu.SemaphoreType.DMA,
        ],
        compiler_params=pltpu.CompilerParams(vmem_limit_bytes=60 * 1024 * 1024),
        name="outer",
    )(pre, rows)


def solution(mesh):
    return jax.shard_map(
        per_device,
        mesh=mesh,
        in_specs=(
            P("expert", "dp"),
            P("expert", "dp"),
            P("expert", None),
            P("expert", None),
            P("expert", None, "dp", None),
        ),
        out_specs=P("expert", None, "dp", None),
        check_vma=False,
    )
```

```python
import functools

import jax
import jax.numpy as jnp
from jax import lax
from jax.experimental import pallas as pl
from jax.experimental.pallas import tpu as pltpu
from jax.sharding import PartitionSpec as P

CAP = 40
CORES = 2
REACH = 2
MESH = pl.DeviceIdType.MESH


def exchange_kernel(
    sizes, tok_ref, cot_ref, routes_ref, gates_ref, w_ref,
    rows_ref, pre_ref,
    buf, metab, wbuf, sel, gsel, rows, acc,
    rsem, zsem, farsem, diagsem, esem, bsem, msem_r, msem_s, osem, wsem, rowsem,
):
    chips, groups, local, per_token, length = sizes
    stages = groups.bit_length() - 1
    dp = lax.axis_index("dp")
    own = lax.axis_index("expert")
    z, core = dp // CORES, dp % CORES
    other = 1 - core
    tokens_each, features = tok_ref.shape
    hidden = w_ref.shape[2]

    def peer(z_to, core_to, group_to):
        return (z_to * CORES + core_to, group_to)

    def across(index, bit):
        return index + bit - 2 * bit * ((index // bit) % 2)

    def mirror(mask):
        result = own
        for place in range(stages):
            if mask >> place & 1:
                result = across(result, 1 << place)
        return result

    own_copies = [
        pltpu.make_async_copy(ref, buf.at[core, a, z, own], osem.at[a])
        for a, ref in enumerate((tok_ref, cot_ref))
    ]
    for copy in own_copies:
        copy.start()
    metab[own] = jnp.zeros(metab.shape[1:], jnp.float32)
    metab[own, 0:per_token] = routes_ref[...].astype(jnp.float32)
    metab[own, per_token:2 * per_token] = gates_ref[...]

    greeted = [
        peer(lax.rem(z + 1, chips), core, own),
        peer(lax.rem(z + chips - 1, chips), core, own),
        peer(z, other, own),
    ] + [peer(z, core, mirror(mask)) for mask in range(1, groups)]
    barrier = pltpu.get_barrier_semaphore()
    for device in greeted:
        pl.semaphore_signal(barrier, inc=1, device_id=device, device_id_type=MESH)
    pl.semaphore_wait(barrier, len(greeted))
    for copy in own_copies:
        copy.wait()

    def send(c, a, zz, s, sem, device):
        return pltpu.make_async_remote_copy(
            src_ref=buf.at[c, a, zz, s], dst_ref=buf.at[c, a, zz, s],
            send_sem=sem, recv_sem=rsem.at[c, a, zz, s],
            device_id=device, device_id_type=MESH,
        )

    def arrived(c, a, zz, s):
        pltpu.make_async_copy(
            buf.at[c, a, zz, s], buf.at[c, a, zz, s], rsem.at[c, a, zz, s]
        ).wait()

    def to_sibling(a, zz, s):
        send(core, a, zz, s, bsem, peer(z, other, own)).start()

    def bit_of(a, stage):
        return 1 << ((stage + a) % stages)

    def mask_list(a, stage):
        masks = [0]
        for earlier in range(stage):
            masks = masks + [mask ^ bit_of(a, earlier) for mask in masks]
        return masks

    def fresh_masks(a, stage):
        return [mask ^ bit_of(a, stage) for mask in mask_list(a, stage)]

    def nearest(k):
        m = jnp.where(2 * z < chips, z, chips - 1 - z)
        side = jnp.where(k % 2 == 1, z - (k + 1) // 2, z + k // 2)
        rest = jnp.where(2 * z < chips, k, chips - 1 - k)
        return jnp.where(k <= 2 * m, side, rest)

    def z_send(zz, a, upward, s=own, sem=zsem):
        return send(
            core, a, zz, s, sem.at[a, zz, 0 if upward else 1],
            peer(z + 1 if upward else z - 1, core, own),
        )

    far = groups - 1
    by_z = stages > 1

    def over_z(zz):
        return (zz != z) & (zz - z <= REACH) & (z - zz <= REACH)

    def far_up(zz):
        return (zz <= z) & (z < chips - 1) & (z + 1 - zz <= REACH)

    def far_down(zz):
        return (zz >= z) & (z > 0) & (zz - z + 1 <= REACH)

    def far_forward(zz, first):
        s = mirror(far)
        for a in range(2):
            if not first:
                arrived(core, a, zz, s)

            @pl.when(far_up(zz))
            def _():
                z_send(zz, a, True, s, farsem).start()

            @pl.when(far_down(zz))
            def _():
                z_send(zz, a, False, s, farsem).start()

            if not first:
                to_sibling(a, zz, s)

    def far_send(zz, a):
        bit = bit_of(a, stages - 1)
        return send(
            core, a, zz, mirror(far ^ bit), diagsem.at[a, zz], peer(z, core, mirror(bit))
        )

    def z_forward(zz, first):
        for a in range(2):
            if not first:
                arrived(core, a, zz, own)

            @pl.when((zz <= z) & (z < chips - 1))
            def _():
                z_send(zz, a, True).start()

            @pl.when((zz >= z) & (z > 0))
            def _():
                z_send(zz, a, False).start()

            to_sibling(a, zz, own)

    def stage_send(k, stage):
        zz = nearest(k)
        for a in range(2):
            if stage > 0:
                for mask in fresh_masks(a, stage - 1):
                    arrived(core, a, zz, mirror(mask))
            for mask in mask_list(a, stage):
                if by_z and stage == stages - 1 and mask == far ^ bit_of(a, stage):
                    @pl.when(jnp.logical_not(over_z(zz)))
                    def _():
                        far_send(zz, a).start()
                    continue
                send(
                    core, a, zz, mirror(mask), esem, peer(z, core, mirror(bit_of(a, stage)))
                ).start()
            if stage > 0:
                for mask in fresh_masks(a, stage - 1):
                    to_sibling(a, zz, mirror(mask))

    def last_arrivals(k):
        zz = nearest(k)
        for a in range(2):
            for mask in fresh_masks(a, stages - 1):
                if by_z and mask == far:
                    @pl.when(jnp.logical_not(over_z(zz)))
                    def _():
                        arrived(core, a, zz, mirror(far))
                        to_sibling(a, zz, mirror(far))
                    continue
                arrived(core, a, zz, mirror(mask))
                to_sibling(a, zz, mirror(mask))

    contract_last = (((1,), (1,)), ((), ()))

    def compute(k):
        zz = nearest(k)
        for turn in range(2):
            c = core if turn == 0 else other
            if turn == 1:
                for a in range(2):
                    for mask in range(groups):
                        arrived(c, a, zz, mirror(mask))
            f = zz * CORES + c
            columns = pl.ds(pl.multiple_of(f * features, features), features)
            x = buf[c, 0, zz].reshape(groups * tokens_each, features)
            y = buf[c, 1, zz].reshape(groups * tokens_each, features)
            pick = sel[...].reshape(local * length, groups * tokens_each)
            rows[f, 0] = (
                jnp.dot(pick, x, preferred_element_type=jnp.float32)
                .astype(jnp.bfloat16).reshape(local, length, features)
            )
            rows[f, 1] = (
                (jnp.dot(pick, y, preferred_element_type=jnp.float32) * gsel[:, :1])
                .astype(jnp.bfloat16).reshape(local, length, features)
            )
            for e in range(local):
                acc[e, 0:2] += lax.dot_general(
                    wbuf[e, 0:2, :, columns].reshape(2 * hidden, features), rows[f, 0, e],
                    contract_last, preferred_element_type=jnp.float32,
                ).reshape(2, hidden, length)
                acc[e, 2] += lax.dot_general(
                    wbuf[e, 2, :, columns], rows[f, 1, e],
                    contract_last, preferred_element_type=jnp.float32,
                )
            pltpu.make_async_copy(rows.at[f], rows_ref.at[f], rowsem).start()

    for mask in range(1, groups):
        pltpu.make_async_remote_copy(
            src_ref=metab.at[own], dst_ref=metab.at[own], send_sem=msem_s,
            recv_sem=msem_r.at[own], device_id=peer(z, core, mirror(mask)),
            device_id_type=MESH,
        ).start()
    stage_send(0, 0)
    z_forward(z, True)
    for e in range(local):
        pltpu.make_async_copy(w_ref.at[e], wbuf.at[e], wsem).start()

    acc[...] = jnp.zeros_like(acc)
    for mask in range(1, groups):
        s = mirror(mask)
        pltpu.make_async_copy(metab.at[s], metab.at[s], msem_r.at[s]).wait()
    triangle = (
        lax.broadcasted_iota(jnp.int32, (tokens_each, tokens_each), 0)
        < lax.broadcasted_iota(jnp.int32, (tokens_each, tokens_each), 1)
    ).astype(jnp.bfloat16)
    slots = lax.broadcasted_iota(jnp.int32, (length, tokens_each), 0).astype(jnp.float32)
    for e in range(local):
        wanted = (own * local + e).astype(jnp.float32)
        opening = jnp.zeros((1, 1), jnp.float32)
        gate_sum = jnp.zeros((length, 1), jnp.float32)
        for s in range(groups):
            table = metab[s]
            hit = jnp.zeros((1, tokens_each), jnp.float32)
            gate = jnp.zeros((1, tokens_each), jnp.float32)
            for k in range(per_token):
                same = table[k:k + 1] == wanted
                hit = jnp.where(same, 1.0, hit)
                gate = jnp.where(same, table[per_token + k:per_token + k + 1], gate)
            wide = jnp.broadcast_to(hit, (16, tokens_each)).astype(jnp.bfloat16)
            place = jnp.dot(wide, triangle, preferred_element_type=jnp.float32)[:1] + opening
            opening = opening + jnp.sum(hit, axis=1, keepdims=True)
            picked = (slots == place) & (hit > 0.5)
            sel[e, :, s * tokens_each:(s + 1) * tokens_each] = jnp.where(
                picked, 1.0, 0.0
            ).astype(jnp.bfloat16)
            gate_sum = gate_sum + jnp.sum(
                jnp.where(picked, gate, 0.0), axis=1, keepdims=True
            )
        gsel[e * length:(e + 1) * length] = jnp.broadcast_to(gate_sum, (length, 128))

    def step(k, carry):
        @pl.when((k > 0) & (k < chips))
        def _():
            @pl.when(z - k >= 0)
            def _():
                z_forward(z - k, False)

            @pl.when(z + k < chips)
            def _():
                z_forward(z + k, False)

            stage_send(k, 0)

        for stage in range(1, stages):
            @pl.when((k >= stage) & (k < chips + stage))
            def _(stage=stage):
                stage_send(k - stage, stage)

        if by_z:
            distance = k - stages

            @pl.when((distance > 0) & (distance <= REACH))
            def _():
                @pl.when(z - distance >= 0)
                def _():
                    far_forward(z - distance, False)

                @pl.when(z + distance < chips)
                def _():
                    far_forward(z + distance, False)

        @pl.when(k == stages + 1)
        def _():
            pltpu.make_async_copy(w_ref, wbuf, wsem).wait()

        @pl.when(k >= stages + 1)
        def _():
            compute(k - stages - 1)

        @pl.when((k >= stages) & (k < chips + stages))
        def _():
            last_arrivals(k - stages)

        if by_z:
            @pl.when(k == stages)
            def _():
                far_forward(z, True)

        return carry

    lax.fori_loop(0, chips + stages + 1, step, 0)

    if pre_ref.shape[-1] > length:
        pre_ref[:, :, :, length:] = jnp.zeros(
            pre_ref.shape[:3] + (pre_ref.shape[-1] - length,), jnp.bfloat16
        )
    for e in range(local):
        gate_part, up_part, back = acc[e, 0], acc[e, 1], acc[e, 2]
        sigmoid = jax.nn.sigmoid(gate_part)
        silu = gate_part * sigmoid
        pre_ref[e, 0, :, :length] = (
            back * up_part * (sigmoid * (1.0 + gate_part * (1.0 - sigmoid)))
        ).astype(jnp.bfloat16)
        pre_ref[e, 1, :, :length] = (back * silu).astype(jnp.bfloat16)
        pre_ref[e, 2, :, :length] = (silu * up_part).astype(jnp.bfloat16)

    def z_drain(zz, carry):
        for a in range(2):
            @pl.when((zz <= z) & (z < chips - 1))
            def _():
                z_send(zz, a, True).wait_send()

            @pl.when((zz >= z) & (z > 0))
            def _():
                z_send(zz, a, False).wait_send()

            if by_z:
                @pl.when(far_up(zz))
                def _():
                    z_send(zz, a, True, mirror(far), farsem).wait_send()

                @pl.when(far_down(zz))
                def _():
                    z_send(zz, a, False, mirror(far), farsem).wait_send()

                @pl.when(jnp.logical_not(over_z(zz)))
                def _():
                    far_send(zz, a).wait_send()

        return carry

    lax.fori_loop(0, chips, z_drain, 0)
    sent = buf.at[0, :, :, pl.ds(0, groups - 2 if by_z else groups - 1)]
    pltpu.make_async_copy(sent, sent, esem).wait()
    pltpu.make_async_copy(buf.at[0], buf.at[0], bsem).wait()
    sent = metab.at[pl.ds(0, groups - 1)]
    pltpu.make_async_copy(sent, sent, msem_s).wait()
    pltpu.make_async_copy(rows, rows_ref, rowsem).wait()


def outer_kernel(
    pieces, length, pre_hbm, rows_ref, out_ref, pre, rbuf, obuf, insem, osem, psem
):
    local, parts, hidden, padded = pre.shape
    devices, features = rbuf.shape[1], rbuf.shape[-1]
    per_expert = devices // pieces
    slots = obuf.shape[0]
    steps = local * per_expert

    def rows_in(e):
        return pltpu.make_async_copy(
            rows_ref.at[:, :, e], rbuf.at[e, :, :, pl.ds(0, length)], insem.at[e]
        )

    def write(step):
        slot = step % slots
        e, j = step // per_expert, step % per_expert
        width = pieces * features
        return pltpu.make_async_copy(
            obuf.at[slot],
            out_ref.at[e, :, :, pl.ds(pl.multiple_of(j * width, width), width)],
            osem.at[slot],
        )

    pre_in = pltpu.make_async_copy(pre_hbm, pre, psem)
    pre_in.start()
    for e in range(local):
        rows_in(e).start()
    if padded > length:
        rbuf[:, :, :, length:] = jnp.zeros(
            rbuf.shape[:3] + (padded - length, features), jnp.bfloat16
        )
    pre_in.wait()

    def one(step, carry):
        slot = step % slots
        e, j = step // per_expert, step % per_expert

        @pl.when(j == 0)
        def _():
            rows_in(e).wait()

        @pl.when(step >= slots)
        def _():
            write(step - slots).wait()

        for piece in range(pieces):
            f = j * pieces + piece
            columns = slice(piece * features, (piece + 1) * features)
            obuf[slot, 0:2, :, columns] = jnp.dot(
                pre[e, 0:2].reshape(2 * hidden, padded), rbuf[e, f, 0],
                preferred_element_type=jnp.float32,
            ).astype(jnp.bfloat16).reshape(2, hidden, features)
            obuf[slot, 2, :, columns] = jnp.dot(
                pre[e, 2], rbuf[e, f, 1], preferred_element_type=jnp.float32
            ).astype(jnp.bfloat16)
        write(step).start()
        return carry

    lax.fori_loop(0, steps, one, 0)
    for step in range(max(0, steps - slots), steps):
        write(step).wait()


def per_device(tokens, cotangent, routes, gates, expert_weights):
    local, parts, hidden, total_features = expert_weights.shape
    tokens_each, features = tokens.shape
    per_token = routes.shape[1]
    groups = lax.axis_size("expert")
    devices = lax.axis_size("dp")
    chips = devices // CORES
    length = groups * CAP
    meta_rows = -(-2 * per_token // 8) * 8
    padded = -(-length // 128) * 128
    sizes = (chips, groups, local, per_token, length)
    any_space = pl.BlockSpec(memory_space=pl.ANY)
    in_vmem = pl.BlockSpec(memory_space=pltpu.VMEM)
    rows, pre = pl.pallas_call(
        functools.partial(exchange_kernel, sizes),
        out_shape=(
            jax.ShapeDtypeStruct((devices, 2, local, length, features), jnp.bfloat16),
            jax.ShapeDtypeStruct((local, parts, hidden, padded), jnp.bfloat16),
        ),
        in_specs=[any_space, any_space, in_vmem, in_vmem, any_space],
        out_specs=(any_space, in_vmem),
        scratch_shapes=[
            pltpu.VMEM((CORES, 2, chips, groups, tokens_each, features), jnp.bfloat16),
            pltpu.VMEM((groups, meta_rows, tokens_each), jnp.float32),
            pltpu.VMEM(expert_weights.shape, jnp.bfloat16),
            pltpu.VMEM((local, length, groups * tokens_each), jnp.bfloat16),
            pltpu.VMEM((local * length, 128), jnp.float32),
            pltpu.VMEM((devices, 2, local, length, features), jnp.bfloat16),
            pltpu.VMEM((local, parts, hidden, length), jnp.float32),
            pltpu.SemaphoreType.DMA((CORES, 2, chips, groups)),
            pltpu.SemaphoreType.DMA((2, chips, 2)),
            pltpu.SemaphoreType.DMA((2, chips, 2)),
            pltpu.SemaphoreType.DMA((2, chips)),
            pltpu.SemaphoreType.DMA,
            pltpu.SemaphoreType.DMA,
            pltpu.SemaphoreType.DMA((groups,)),
            pltpu.SemaphoreType.DMA,
            pltpu.SemaphoreType.DMA((2,)),
            pltpu.SemaphoreType.DMA,
            pltpu.SemaphoreType.DMA,
        ],
        compiler_params=pltpu.CompilerParams(
            collective_id=0, has_side_effects=True, vmem_limit_bytes=60 * 1024 * 1024
        ),
        name="exchange",
    )(tokens, cotangent, routes.T, gates.T, expert_weights)
    pieces = max(1, devices // 4)
    slots = 5
    return pl.pallas_call(
        functools.partial(outer_kernel, pieces, length),
        out_shape=jax.ShapeDtypeStruct(expert_weights.shape, jnp.bfloat16),
        in_specs=[any_space] * 2,
        out_specs=any_space,
        scratch_shapes=[
            pltpu.VMEM((local, parts, hidden, padded), jnp.bfloat16),
            pltpu.VMEM((local, devices, 2, padded, features), jnp.bfloat16),
            pltpu.VMEM((slots, parts, hidden, pieces * features), jnp.bfloat16),
            pltpu.SemaphoreType.DMA((local,)),
            pltpu.SemaphoreType.DMA((slots,)),
            pltpu.SemaphoreType.DMA,
        ],
        compiler_params=pltpu.CompilerParams(vmem_limit_bytes=60 * 1024 * 1024),
        name="outer",
    )(pre, rows)


def solution(mesh):
    return jax.shard_map(
        per_device,
        mesh=mesh,
        in_specs=(
            P("expert", "dp"),
            P("expert", "dp"),
            P("expert", None),
            P("expert", None),
            P("expert", None, "dp", None),
        ),
        out_specs=P("expert", None, "dp", None),
        check_vma=False,
    )
```

```python
import functools

import jax
import jax.numpy as jnp
from jax import lax
from jax.experimental import pallas as pl
from jax.experimental.pallas import tpu as pltpu
from jax.sharding import PartitionSpec as P

CAP = 40
CORES = 2
REACH = 2
MESH = pl.DeviceIdType.MESH


def exchange_kernel(
    sizes, tok_ref, cot_ref, routes_ref, gates_ref, w_ref,
    rows_ref, pre_ref,
    buf, metab, wbuf, sel, gsel, rows, acc,
    rsem, zsem, farsem, diagsem, esem, bsem, msem_r, msem_s, osem, wsem, rowsem,
):
    chips, groups, local, per_token, length = sizes
    stages = groups.bit_length() - 1
    dp = lax.axis_index("dp")
    own = lax.axis_index("expert")
    z, core = dp // CORES, dp % CORES
    other = 1 - core
    tokens_each, features = tok_ref.shape
    hidden = w_ref.shape[2]

    def peer(z_to, core_to, group_to):
        return (z_to * CORES + core_to, group_to)

    def across(index, bit):
        return index + bit - 2 * bit * ((index // bit) % 2)

    def mirror(mask):
        result = own
        for place in range(stages):
            if mask >> place & 1:
                result = across(result, 1 << place)
        return result

    own_copies = [
        pltpu.make_async_copy(ref, buf.at[core, a, z, own], osem.at[a])
        for a, ref in enumerate((tok_ref, cot_ref))
    ]
    for copy in own_copies:
        copy.start()
    metab[own] = jnp.zeros(metab.shape[1:], jnp.float32)
    metab[own, 0:per_token] = routes_ref[...].astype(jnp.float32)
    metab[own, per_token:2 * per_token] = gates_ref[...]

    greeted = [
        peer(lax.rem(z + 1, chips), core, own),
        peer(lax.rem(z + chips - 1, chips), core, own),
        peer(z, other, own),
    ] + [peer(z, core, mirror(mask)) for mask in range(1, groups)]
    barrier = pltpu.get_barrier_semaphore()
    for device in greeted:
        pl.semaphore_signal(barrier, inc=1, device_id=device, device_id_type=MESH)
    pl.semaphore_wait(barrier, len(greeted))
    for copy in own_copies:
        copy.wait()

    def send(c, a, zz, s, sem, device):
        return pltpu.make_async_remote_copy(
            src_ref=buf.at[c, a, zz, s], dst_ref=buf.at[c, a, zz, s],
            send_sem=sem, recv_sem=rsem.at[c, a, zz, s],
            device_id=device, device_id_type=MESH,
        )

    def arrived(c, a, zz, s):
        pltpu.make_async_copy(
            buf.at[c, a, zz, s], buf.at[c, a, zz, s], rsem.at[c, a, zz, s]
        ).wait()

    def to_sibling(a, zz, s):
        send(core, a, zz, s, bsem, peer(z, other, own)).start()

    def bit_of(a, stage):
        return 1 << ((stage + a) % stages)

    def mask_list(a, stage):
        masks = [0]
        for earlier in range(stage):
            masks = masks + [mask ^ bit_of(a, earlier) for mask in masks]
        return masks

    def fresh_masks(a, stage):
        return [mask ^ bit_of(a, stage) for mask in mask_list(a, stage)]

    def nearest(k):
        m = jnp.where(2 * z < chips, z, chips - 1 - z)
        side = jnp.where(k % 2 == 1, z - (k + 1) // 2, z + k // 2)
        rest = jnp.where(2 * z < chips, k, chips - 1 - k)
        return jnp.where(k <= 2 * m, side, rest)

    def z_send(zz, a, upward, s=own, sem=zsem):
        return send(
            core, a, zz, s, sem.at[a, zz, 0 if upward else 1],
            peer(z + 1 if upward else z - 1, core, own),
        )

    far = groups - 1
    by_z = stages > 1

    def over_z(zz):
        return (zz != z) & (zz - z <= REACH) & (z - zz <= REACH)

    def far_up(zz):
        return (zz <= z) & (z < chips - 1) & (z + 1 - zz <= REACH)

    def far_down(zz):
        return (zz >= z) & (z > 0) & (zz - z + 1 <= REACH)

    def far_forward(zz, first):
        s = mirror(far)
        for a in range(2):
            if not first:
                arrived(core, a, zz, s)

            @pl.when(far_up(zz))
            def _():
                z_send(zz, a, True, s, farsem).start()

            @pl.when(far_down(zz))
            def _():
                z_send(zz, a, False, s, farsem).start()

            if not first:
                to_sibling(a, zz, s)

    def far_send(zz, a):
        bit = bit_of(a, stages - 1)
        return send(
            core, a, zz, mirror(far ^ bit), diagsem.at[a, zz], peer(z, core, mirror(bit))
        )

    def z_forward(zz, first):
        for a in range(2):
            if not first:
                arrived(core, a, zz, own)

            @pl.when((zz <= z) & (z < chips - 1))
            def _():
                z_send(zz, a, True).start()

            @pl.when((zz >= z) & (z > 0))
            def _():
                z_send(zz, a, False).start()

            to_sibling(a, zz, own)

    def stage_send(k, stage):
        zz = nearest(k)
        for a in range(2):
            if stage > 0:
                for mask in fresh_masks(a, stage - 1):
                    arrived(core, a, zz, mirror(mask))
            for mask in mask_list(a, stage):
                if by_z and stage == stages - 1 and mask == far ^ bit_of(a, stage):
                    @pl.when(jnp.logical_not(over_z(zz)))
                    def _():
                        far_send(zz, a).start()
                    continue
                send(
                    core, a, zz, mirror(mask), esem, peer(z, core, mirror(bit_of(a, stage)))
                ).start()
            if stage > 0:
                for mask in fresh_masks(a, stage - 1):
                    to_sibling(a, zz, mirror(mask))

    def last_arrivals(k):
        zz = nearest(k)
        for a in range(2):
            for mask in fresh_masks(a, stages - 1):
                if by_z and mask == far:
                    @pl.when(jnp.logical_not(over_z(zz)))
                    def _():
                        arrived(core, a, zz, mirror(far))
                        to_sibling(a, zz, mirror(far))
                    continue
                arrived(core, a, zz, mirror(mask))
                to_sibling(a, zz, mirror(mask))

    contract_last = (((1,), (1,)), ((), ()))

    def compute(k):
        zz = nearest(k)
        for turn in range(2):
            c = core if turn == 0 else other
            if turn == 1:
                for a in range(2):
                    for mask in range(groups):
                        arrived(c, a, zz, mirror(mask))
            f = zz * CORES + c
            columns = pl.ds(pl.multiple_of(f * features, features), features)
            x = buf[c, 0, zz].reshape(groups * tokens_each, features)
            y = buf[c, 1, zz].reshape(groups * tokens_each, features)
            pick = sel[...].reshape(local * length, groups * tokens_each)
            rows[f, 0] = (
                jnp.dot(pick, x, preferred_element_type=jnp.float32)
                .astype(jnp.bfloat16).reshape(local, length, features)
            )
            rows[f, 1] = (
                (jnp.dot(pick, y, preferred_element_type=jnp.float32) * gsel[:, :1])
                .astype(jnp.bfloat16).reshape(local, length, features)
            )
            for e in range(local):
                acc[e, 0:2] += lax.dot_general(
                    wbuf[e, 0:2, :, columns].reshape(2 * hidden, features), rows[f, 0, e],
                    contract_last, preferred_element_type=jnp.float32,
                ).reshape(2, hidden, length)
                acc[e, 2] += lax.dot_general(
                    wbuf[e, 2, :, columns], rows[f, 1, e],
                    contract_last, preferred_element_type=jnp.float32,
                )
            pltpu.make_async_copy(rows.at[f], rows_ref.at[f], rowsem).start()

    for mask in range(1, groups):
        pltpu.make_async_remote_copy(
            src_ref=metab.at[own], dst_ref=metab.at[own], send_sem=msem_s,
            recv_sem=msem_r.at[own], device_id=peer(z, core, mirror(mask)),
            device_id_type=MESH,
        ).start()
    stage_send(0, 0)
    z_forward(z, True)
    for e in range(local):
        pltpu.make_async_copy(w_ref.at[e], wbuf.at[e], wsem).start()

    acc[...] = jnp.zeros_like(acc)
    for mask in range(1, groups):
        s = mirror(mask)
        pltpu.make_async_copy(metab.at[s], metab.at[s], msem_r.at[s]).wait()
    triangle = (
        lax.broadcasted_iota(jnp.int32, (tokens_each, tokens_each), 0)
        < lax.broadcasted_iota(jnp.int32, (tokens_each, tokens_each), 1)
    ).astype(jnp.bfloat16)
    slots = lax.broadcasted_iota(jnp.int32, (length, tokens_each), 0).astype(jnp.float32)
    for e in range(local):
        wanted = (own * local + e).astype(jnp.float32)
        opening = jnp.zeros((1, 1), jnp.float32)
        gate_sum = jnp.zeros((length, 1), jnp.float32)
        for s in range(groups):
            table = metab[s]
            hit = jnp.zeros((1, tokens_each), jnp.float32)
            gate = jnp.zeros((1, tokens_each), jnp.float32)
            for k in range(per_token):
                same = table[k:k + 1] == wanted
                hit = jnp.where(same, 1.0, hit)
                gate = jnp.where(same, table[per_token + k:per_token + k + 1], gate)
            wide = jnp.broadcast_to(hit, (16, tokens_each)).astype(jnp.bfloat16)
            place = jnp.dot(wide, triangle, preferred_element_type=jnp.float32)[:1] + opening
            opening = opening + jnp.sum(hit, axis=1, keepdims=True)
            picked = (slots == place) & (hit > 0.5)
            sel[e, :, s * tokens_each:(s + 1) * tokens_each] = jnp.where(
                picked, 1.0, 0.0
            ).astype(jnp.bfloat16)
            gate_sum = gate_sum + jnp.sum(
                jnp.where(picked, gate, 0.0), axis=1, keepdims=True
            )
        gsel[e * length:(e + 1) * length] = jnp.broadcast_to(gate_sum, (length, 128))

    def step(k, carry):
        @pl.when(k == stages + 1)
        def _():
            pltpu.make_async_copy(w_ref, wbuf, wsem).wait()

        @pl.when(k >= stages + 1)
        def _():
            compute(k - stages - 1)

        @pl.when((k > 0) & (k < chips))
        def _():
            @pl.when(z - k >= 0)
            def _():
                z_forward(z - k, False)

            @pl.when(z + k < chips)
            def _():
                z_forward(z + k, False)

            stage_send(k, 0)

        for stage in range(1, stages):
            @pl.when((k >= stage) & (k < chips + stage))
            def _(stage=stage):
                stage_send(k - stage, stage)

        if by_z:
            distance = k - stages

            @pl.when((distance > 0) & (distance <= REACH))
            def _():
                @pl.when(z - distance >= 0)
                def _():
                    far_forward(z - distance, False)

                @pl.when(z + distance < chips)
                def _():
                    far_forward(z + distance, False)

        @pl.when((k >= stages) & (k < chips + stages))
        def _():
            last_arrivals(k - stages)

        if by_z:
            @pl.when(k == stages)
            def _():
                far_forward(z, True)

        return carry

    lax.fori_loop(0, chips + stages + 1, step, 0)

    if pre_ref.shape[-1] > length:
        pre_ref[:, :, :, length:] = jnp.zeros(
            pre_ref.shape[:3] + (pre_ref.shape[-1] - length,), jnp.bfloat16
        )
    for e in range(local):
        gate_part, up_part, back = acc[e, 0], acc[e, 1], acc[e, 2]
        sigmoid = jax.nn.sigmoid(gate_part)
        silu = gate_part * sigmoid
        pre_ref[e, 0, :, :length] = (
            back * up_part * (sigmoid * (1.0 + gate_part * (1.0 - sigmoid)))
        ).astype(jnp.bfloat16)
        pre_ref[e, 1, :, :length] = (back * silu).astype(jnp.bfloat16)
        pre_ref[e, 2, :, :length] = (silu * up_part).astype(jnp.bfloat16)

    def z_drain(zz, carry):
        for a in range(2):
            @pl.when((zz <= z) & (z < chips - 1))
            def _():
                z_send(zz, a, True).wait_send()

            @pl.when((zz >= z) & (z > 0))
            def _():
                z_send(zz, a, False).wait_send()

            if by_z:
                @pl.when(far_up(zz))
                def _():
                    z_send(zz, a, True, mirror(far), farsem).wait_send()

                @pl.when(far_down(zz))
                def _():
                    z_send(zz, a, False, mirror(far), farsem).wait_send()

                @pl.when(jnp.logical_not(over_z(zz)))
                def _():
                    far_send(zz, a).wait_send()

        return carry

    lax.fori_loop(0, chips, z_drain, 0)
    sent = buf.at[0, :, :, pl.ds(0, groups - 2 if by_z else groups - 1)]
    pltpu.make_async_copy(sent, sent, esem).wait()
    pltpu.make_async_copy(buf.at[0], buf.at[0], bsem).wait()
    sent = metab.at[pl.ds(0, groups - 1)]
    pltpu.make_async_copy(sent, sent, msem_s).wait()
    pltpu.make_async_copy(rows, rows_ref, rowsem).wait()


def outer_kernel(
    pieces, length, pre_hbm, rows_ref, out_ref, pre, rbuf, obuf, insem, osem, psem
):
    local, parts, hidden, padded = pre.shape
    devices, features = rbuf.shape[1], rbuf.shape[-1]
    per_expert = devices // pieces
    slots = obuf.shape[0]
    steps = local * per_expert

    def rows_in(step):
        e, first = step // per_expert, step % per_expert * pieces
        return pltpu.make_async_copy(
            rows_ref.at[pl.ds(first, pieces), :, e],
            rbuf.at[e, pl.ds(first, pieces), :, pl.ds(0, length)], insem.at[step],
        )

    def pre_in(e):
        return pltpu.make_async_copy(pre_hbm.at[e], pre.at[e], psem.at[e])

    def write(step):
        slot = step % slots
        e, j = step // per_expert, step % per_expert
        width = pieces * features
        return pltpu.make_async_copy(
            obuf.at[slot],
            out_ref.at[e, :, :, pl.ds(pl.multiple_of(j * width, width), width)],
            osem.at[slot],
        )

    pre_in(0).start()
    ahead = min(4, steps)
    for step in range(ahead):
        rows_in(step).start()
    for e in range(1, local):
        pre_in(e).start()
    if padded > length:
        rbuf[:, :, :, length:] = jnp.zeros(
            rbuf.shape[:3] + (padded - length, features), jnp.bfloat16
        )
    def one(step, carry):
        slot = step % slots
        e, j = step // per_expert, step % per_expert

        @pl.when(j == 0)
        def _():
            pre_in(e).wait()

        rows_in(step).wait()

        @pl.when(step + ahead < steps)
        def _():
            rows_in(step + ahead).start()

        @pl.when(step >= slots)
        def _():
            write(step - slots).wait()

        for piece in range(pieces):
            f = j * pieces + piece
            columns = slice(piece * features, (piece + 1) * features)
            obuf[slot, 0:2, :, columns] = jnp.dot(
                pre[e, 0:2].reshape(2 * hidden, padded), rbuf[e, f, 0],
                preferred_element_type=jnp.float32,
            ).astype(jnp.bfloat16).reshape(2, hidden, features)
            obuf[slot, 2, :, columns] = jnp.dot(
                pre[e, 2], rbuf[e, f, 1], preferred_element_type=jnp.float32
            ).astype(jnp.bfloat16)
        write(step).start()
        return carry

    lax.fori_loop(0, steps, one, 0)
    for step in range(max(0, steps - slots), steps):
        write(step).wait()


def per_device(tokens, cotangent, routes, gates, expert_weights):
    local, parts, hidden, total_features = expert_weights.shape
    tokens_each, features = tokens.shape
    per_token = routes.shape[1]
    groups = lax.axis_size("expert")
    devices = lax.axis_size("dp")
    chips = devices // CORES
    length = groups * CAP
    meta_rows = -(-2 * per_token // 8) * 8
    padded = -(-length // 128) * 128
    sizes = (chips, groups, local, per_token, length)
    any_space = pl.BlockSpec(memory_space=pl.ANY)
    in_vmem = pl.BlockSpec(memory_space=pltpu.VMEM)
    rows, pre = pl.pallas_call(
        functools.partial(exchange_kernel, sizes),
        out_shape=(
            jax.ShapeDtypeStruct((devices, 2, local, length, features), jnp.bfloat16),
            jax.ShapeDtypeStruct((local, parts, hidden, padded), jnp.bfloat16),
        ),
        in_specs=[any_space, any_space, in_vmem, in_vmem, any_space],
        out_specs=(any_space, in_vmem),
        scratch_shapes=[
            pltpu.VMEM((CORES, 2, chips, groups, tokens_each, features), jnp.bfloat16),
            pltpu.VMEM((groups, meta_rows, tokens_each), jnp.float32),
            pltpu.VMEM(expert_weights.shape, jnp.bfloat16),
            pltpu.VMEM((local, length, groups * tokens_each), jnp.bfloat16),
            pltpu.VMEM((local * length, 128), jnp.float32),
            pltpu.VMEM((devices, 2, local, length, features), jnp.bfloat16),
            pltpu.VMEM((local, parts, hidden, length), jnp.float32),
            pltpu.SemaphoreType.DMA((CORES, 2, chips, groups)),
            pltpu.SemaphoreType.DMA((2, chips, 2)),
            pltpu.SemaphoreType.DMA((2, chips, 2)),
            pltpu.SemaphoreType.DMA((2, chips)),
            pltpu.SemaphoreType.DMA,
            pltpu.SemaphoreType.DMA,
            pltpu.SemaphoreType.DMA((groups,)),
            pltpu.SemaphoreType.DMA,
            pltpu.SemaphoreType.DMA((2,)),
            pltpu.SemaphoreType.DMA,
            pltpu.SemaphoreType.DMA,
        ],
        compiler_params=pltpu.CompilerParams(
            collective_id=0, has_side_effects=True, vmem_limit_bytes=60 * 1024 * 1024
        ),
        name="exchange",
    )(tokens, cotangent, routes.T, gates.T, expert_weights)
    pieces = max(1, devices // 4)
    slots = 5
    return pl.pallas_call(
        functools.partial(outer_kernel, pieces, length),
        out_shape=jax.ShapeDtypeStruct(expert_weights.shape, jnp.bfloat16),
        in_specs=[any_space] * 2,
        out_specs=any_space,
        scratch_shapes=[
            pltpu.VMEM((local, parts, hidden, padded), jnp.bfloat16),
            pltpu.VMEM((local, devices, 2, padded, features), jnp.bfloat16),
            pltpu.VMEM((slots, parts, hidden, pieces * features), jnp.bfloat16),
            pltpu.SemaphoreType.DMA((local * (devices // pieces),)),
            pltpu.SemaphoreType.DMA((slots,)),
            pltpu.SemaphoreType.DMA((local,)),
        ],
        compiler_params=pltpu.CompilerParams(vmem_limit_bytes=60 * 1024 * 1024),
        name="outer",
    )(pre, rows)


def solution(mesh):
    return jax.shard_map(
        per_device,
        mesh=mesh,
        in_specs=(
            P("expert", "dp"),
            P("expert", "dp"),
            P("expert", None),
            P("expert", None),
            P("expert", None, "dp", None),
        ),
        out_specs=P("expert", None, "dp", None),
        check_vma=False,
    )
```

```python
import functools

import jax
import jax.numpy as jnp
from jax import lax
from jax.experimental import pallas as pl
from jax.experimental.pallas import tpu as pltpu
from jax.sharding import PartitionSpec as P

CAP = 40
CORES = 2
REACH = 2
MESH = pl.DeviceIdType.MESH


def exchange_kernel(
    sizes, tok_ref, cot_ref, routes_ref, gates_ref, w_ref,
    rows_ref, pre_ref,
    buf, metab, wbuf, sel, gsel, rows, acc,
    rsem, zsem, farsem, diagsem, esem, bsem, msem_r, msem_s, osem, wsem, rowsem,
):
    chips, groups, local, per_token, length = sizes
    stages = groups.bit_length() - 1
    dp = lax.axis_index("dp")
    own = lax.axis_index("expert")
    z, core = dp // CORES, dp % CORES
    other = 1 - core
    tokens_each = tok_ref.shape[0]
    features = buf.shape[-1]
    halves = tok_ref.shape[1] // features
    count = chips * halves
    hidden = w_ref.shape[2]

    def peer(z_to, core_to, group_to):
        return (z_to * CORES + core_to, group_to)

    def across(index, bit):
        return index + bit - 2 * bit * ((index // bit) % 2)

    def mirror(mask):
        result = own
        for place in range(stages):
            if mask >> place & 1:
                result = across(result, 1 << place)
        return result

    own_copies = [
        pltpu.make_async_copy(
            ref.at[:, half * features:(half + 1) * features],
            buf.at[core, a, z * halves + half, own], osem.at[a, half],
        )
        for a, ref in enumerate((tok_ref, cot_ref)) for half in range(halves)
    ]
    for copy in own_copies:
        copy.start()
    metab[own] = jnp.zeros(metab.shape[1:], jnp.float32)
    metab[own, 0:per_token] = routes_ref[...].astype(jnp.float32)
    metab[own, per_token:2 * per_token] = gates_ref[...]

    greeted = [
        peer(lax.rem(z + 1, chips), core, own),
        peer(lax.rem(z + chips - 1, chips), core, own),
        peer(z, other, own),
    ] + [peer(z, core, mirror(mask)) for mask in range(1, groups)]
    barrier = pltpu.get_barrier_semaphore()
    for device in greeted:
        pl.semaphore_signal(barrier, inc=1, device_id=device, device_id_type=MESH)
    pl.semaphore_wait(barrier, len(greeted))
    for copy in own_copies:
        copy.wait()

    def send(c, a, zz, s, sem, device):
        return pltpu.make_async_remote_copy(
            src_ref=buf.at[c, a, zz, s], dst_ref=buf.at[c, a, zz, s],
            send_sem=sem, recv_sem=rsem.at[c, a, zz, s],
            device_id=device, device_id_type=MESH,
        )

    def arrived(c, a, zz, s):
        pltpu.make_async_copy(
            buf.at[c, a, zz, s], buf.at[c, a, zz, s], rsem.at[c, a, zz, s]
        ).wait()

    def to_sibling(a, zz, s):
        send(core, a, zz, s, bsem, peer(z, other, own)).start()

    def bit_of(a, stage):
        return 1 << ((stage + a) % stages)

    def mask_list(a, stage):
        masks = [0]
        for earlier in range(stage):
            masks = masks + [mask ^ bit_of(a, earlier) for mask in masks]
        return masks

    def fresh_masks(a, stage):
        return [mask ^ bit_of(a, stage) for mask in mask_list(a, stage)]

    def nearest(slot):
        k = slot // halves
        m = jnp.where(2 * z < chips, z, chips - 1 - z)
        side = jnp.where(k % 2 == 1, z - (k + 1) // 2, z + k // 2)
        rest = jnp.where(2 * z < chips, k, chips - 1 - k)
        return jnp.where(k <= 2 * m, side, rest) * halves + slot % halves

    def z_send(zz, a, upward, s=own, sem=zsem):
        return send(
            core, a, zz, s, sem.at[a, zz, 0 if upward else 1],
            peer(z + 1 if upward else z - 1, core, own),
        )

    far = groups - 1
    by_z = stages > 1

    def over_z(block):
        zz = block // halves
        return (zz != z) & (zz - z <= REACH) & (z - zz <= REACH)

    def far_up(block):
        zz = block // halves
        return (zz <= z) & (z < chips - 1) & (z + 1 - zz <= REACH)

    def far_down(block):
        zz = block // halves
        return (zz >= z) & (z > 0) & (zz - z + 1 <= REACH)

    def far_forward(chip, first):
        s = mirror(far)
        for half, a in halves_and_arrays:
            zz = chip * halves + half
            if not first:
                arrived(core, a, zz, s)

            @pl.when(far_up(zz))
            def _():
                z_send(zz, a, True, s, farsem).start()

            @pl.when(far_down(zz))
            def _():
                z_send(zz, a, False, s, farsem).start()

            if not first:
                to_sibling(a, zz, s)

    def far_send(zz, a):
        bit = bit_of(a, stages - 1)
        return send(
            core, a, zz, mirror(far ^ bit), diagsem.at[a, zz], peer(z, core, mirror(bit))
        )

    halves_and_arrays = [(half, a) for half in range(halves) for a in range(2)]

    def own_up(block):
        return (block // halves <= z) & (z < chips - 1)

    def own_down(block):
        return (block // halves >= z) & (z > 0)

    def z_forward(chip, first):
        for half, a in halves_and_arrays:
            zz = chip * halves + half
            if not first:
                arrived(core, a, zz, own)

            @pl.when(own_up(zz))
            def _():
                z_send(zz, a, True).start()

            @pl.when(own_down(zz))
            def _():
                z_send(zz, a, False).start()

            to_sibling(a, zz, own)

    def stage_send(k, stage):
        zz = nearest(k)
        for a in range(2):
            if stage > 0:
                for mask in fresh_masks(a, stage - 1):
                    arrived(core, a, zz, mirror(mask))
            for mask in mask_list(a, stage):
                if by_z and stage == stages - 1 and mask == far ^ bit_of(a, stage):
                    @pl.when(jnp.logical_not(over_z(zz)))
                    def _():
                        far_send(zz, a).start()
                    continue
                send(
                    core, a, zz, mirror(mask), esem, peer(z, core, mirror(bit_of(a, stage)))
                ).start()
            if stage > 0:
                for mask in fresh_masks(a, stage - 1):
                    to_sibling(a, zz, mirror(mask))

    def last_arrivals(k):
        zz = nearest(k)
        for a in range(2):
            for mask in fresh_masks(a, stages - 1):
                if by_z and mask == far:
                    @pl.when(jnp.logical_not(over_z(zz)))
                    def _():
                        arrived(core, a, zz, mirror(far))
                        to_sibling(a, zz, mirror(far))
                    continue
                arrived(core, a, zz, mirror(mask))
                to_sibling(a, zz, mirror(mask))

    contract_last = (((1,), (1,)), ((), ()))

    def compute(k):
        zz = nearest(k)
        for turn in range(2):
            c = core if turn == 0 else other
            if turn == 1:
                for a in range(2):
                    for mask in range(groups):
                        arrived(c, a, zz, mirror(mask))
            f = (zz // halves * CORES + c) * halves + zz % halves
            columns = pl.ds(pl.multiple_of(f * features, features), features)
            x = buf[c, 0, zz].reshape(groups * tokens_each, features)
            y = buf[c, 1, zz].reshape(groups * tokens_each, features)
            pick = sel[...].reshape(local * length, groups * tokens_each)
            rows[f, 0] = (
                jnp.dot(pick, x, preferred_element_type=jnp.float32)
                .astype(jnp.bfloat16).reshape(local, length, features)
            )
            rows[f, 1] = (
                (jnp.dot(pick, y, preferred_element_type=jnp.float32) * gsel[:, :1])
                .astype(jnp.bfloat16).reshape(local, length, features)
            )
            for e in range(local):
                acc[e, 0:2] += lax.dot_general(
                    wbuf[e, 0:2, :, columns].reshape(2 * hidden, features), rows[f, 0, e],
                    contract_last, preferred_element_type=jnp.float32,
                ).reshape(2, hidden, length)
                acc[e, 2] += lax.dot_general(
                    wbuf[e, 2, :, columns], rows[f, 1, e],
                    contract_last, preferred_element_type=jnp.float32,
                )
            pltpu.make_async_copy(rows.at[f], rows_ref.at[f], rowsem).start()

    for mask in range(1, groups):
        pltpu.make_async_remote_copy(
            src_ref=metab.at[own], dst_ref=metab.at[own], send_sem=msem_s,
            recv_sem=msem_r.at[own], device_id=peer(z, core, mirror(mask)),
            device_id_type=MESH,
        ).start()
    for half in range(halves):
        stage_send(half, 0)
    z_forward(z, True)
    for e in range(local):
        pltpu.make_async_copy(w_ref.at[e], wbuf.at[e], wsem).start()

    acc[...] = jnp.zeros_like(acc)
    for mask in range(1, groups):
        s = mirror(mask)
        pltpu.make_async_copy(metab.at[s], metab.at[s], msem_r.at[s]).wait()
    triangle = (
        lax.broadcasted_iota(jnp.int32, (tokens_each, tokens_each), 0)
        < lax.broadcasted_iota(jnp.int32, (tokens_each, tokens_each), 1)
    ).astype(jnp.bfloat16)
    slots = lax.broadcasted_iota(jnp.int32, (length, tokens_each), 0).astype(jnp.float32)
    for e in range(local):
        wanted = (own * local + e).astype(jnp.float32)
        opening = jnp.zeros((1, 1), jnp.float32)
        gate_sum = jnp.zeros((length, 1), jnp.float32)
        for s in range(groups):
            table = metab[s]
            hit = jnp.zeros((1, tokens_each), jnp.float32)
            gate = jnp.zeros((1, tokens_each), jnp.float32)
            for k in range(per_token):
                same = table[k:k + 1] == wanted
                hit = jnp.where(same, 1.0, hit)
                gate = jnp.where(same, table[per_token + k:per_token + k + 1], gate)
            wide = jnp.broadcast_to(hit, (16, tokens_each)).astype(jnp.bfloat16)
            place = jnp.dot(wide, triangle, preferred_element_type=jnp.float32)[:1] + opening
            opening = opening + jnp.sum(hit, axis=1, keepdims=True)
            picked = (slots == place) & (hit > 0.5)
            sel[e, :, s * tokens_each:(s + 1) * tokens_each] = jnp.where(
                picked, 1.0, 0.0
            ).astype(jnp.bfloat16)
            gate_sum = gate_sum + jnp.sum(
                jnp.where(picked, gate, 0.0), axis=1, keepdims=True
            )
        gsel[e * length:(e + 1) * length] = jnp.broadcast_to(gate_sum, (length, 128))

    def step(k, carry):
        @pl.when(k == stages + 1)
        def _():
            pltpu.make_async_copy(w_ref, wbuf, wsem).wait()

        @pl.when(k >= stages + 1)
        def _():
            compute(k - stages - 1)

        distance = k // halves

        @pl.when((k > 0) & (k < count) & (k % halves == 0))
        def _():
            @pl.when(z - distance >= 0)
            def _():
                z_forward(z - distance, False)

            @pl.when(z + distance < chips)
            def _():
                z_forward(z + distance, False)

            for half in range(halves):
                stage_send(k + half, 0)

        for stage in range(1, stages):
            @pl.when((k >= stage) & (k < count + stage))
            def _(stage=stage):
                stage_send(k - stage, stage)

        if by_z:
            reach = (k - stages) // halves

            @pl.when(
                (k >= stages + halves) & (reach <= REACH) & ((k - stages) % halves == 0)
            )
            def _():
                @pl.when(z - reach >= 0)
                def _():
                    far_forward(z - reach, False)

                @pl.when(z + reach < chips)
                def _():
                    far_forward(z + reach, False)

        @pl.when((k >= stages) & (k < count + stages))
        def _():
            last_arrivals(k - stages)

        if by_z:
            @pl.when(k == stages + halves - 1)
            def _():
                far_forward(z, True)

        return carry

    lax.fori_loop(0, count + stages + 1, step, 0)

    if pre_ref.shape[-1] > length:
        pre_ref[:, :, :, length:] = jnp.zeros(
            pre_ref.shape[:3] + (pre_ref.shape[-1] - length,), jnp.bfloat16
        )
    for e in range(local):
        gate_part, up_part, back = acc[e, 0], acc[e, 1], acc[e, 2]
        sigmoid = jax.nn.sigmoid(gate_part)
        silu = gate_part * sigmoid
        pre_ref[e, 0, :, :length] = (
            back * up_part * (sigmoid * (1.0 + gate_part * (1.0 - sigmoid)))
        ).astype(jnp.bfloat16)
        pre_ref[e, 1, :, :length] = (back * silu).astype(jnp.bfloat16)
        pre_ref[e, 2, :, :length] = (silu * up_part).astype(jnp.bfloat16)

    def z_drain(zz, carry):
        for a in range(2):
            @pl.when(own_up(zz))
            def _():
                z_send(zz, a, True).wait_send()

            @pl.when(own_down(zz))
            def _():
                z_send(zz, a, False).wait_send()

            if by_z:
                @pl.when(far_up(zz))
                def _():
                    z_send(zz, a, True, mirror(far), farsem).wait_send()

                @pl.when(far_down(zz))
                def _():
                    z_send(zz, a, False, mirror(far), farsem).wait_send()

                @pl.when(jnp.logical_not(over_z(zz)))
                def _():
                    far_send(zz, a).wait_send()

        return carry

    lax.fori_loop(0, count, z_drain, 0)
    sent = buf.at[0, :, :, pl.ds(0, groups - 2 if by_z else groups - 1)]
    pltpu.make_async_copy(sent, sent, esem).wait()
    pltpu.make_async_copy(buf.at[0], buf.at[0], bsem).wait()
    sent = metab.at[pl.ds(0, groups - 1)]
    pltpu.make_async_copy(sent, sent, msem_s).wait()
    pltpu.make_async_copy(rows, rows_ref, rowsem).wait()


def outer_kernel(
    pieces, length, pre_hbm, rows_ref, out_ref, pre, rbuf, obuf, insem, osem, psem
):
    local, parts, hidden, padded = pre.shape
    devices, features = rbuf.shape[1], rbuf.shape[-1]
    per_expert = devices // pieces
    slots = obuf.shape[0]
    steps = local * per_expert

    def rows_in(step):
        e, first = step // per_expert, step % per_expert * pieces
        return pltpu.make_async_copy(
            rows_ref.at[pl.ds(first, pieces), :, e],
            rbuf.at[e, pl.ds(first, pieces), :, pl.ds(0, length)], insem.at[step],
        )

    def pre_in(e):
        return pltpu.make_async_copy(pre_hbm.at[e], pre.at[e], psem.at[e])

    def write(step):
        slot = step % slots
        e, j = step // per_expert, step % per_expert
        width = pieces * features
        return pltpu.make_async_copy(
            obuf.at[slot],
            out_ref.at[e, :, :, pl.ds(pl.multiple_of(j * width, width), width)],
            osem.at[slot],
        )

    pre_in(0).start()
    ahead = min(4, steps)
    for step in range(ahead):
        rows_in(step).start()
    for e in range(1, local):
        pre_in(e).start()
    if padded > length:
        rbuf[:, :, :, length:] = jnp.zeros(
            rbuf.shape[:3] + (padded - length, features), jnp.bfloat16
        )
    def one(step, carry):
        slot = step % slots
        e, j = step // per_expert, step % per_expert

        @pl.when(j == 0)
        def _():
            pre_in(e).wait()

        rows_in(step).wait()

        @pl.when(step + ahead < steps)
        def _():
            rows_in(step + ahead).start()

        @pl.when(step >= slots)
        def _():
            write(step - slots).wait()

        for piece in range(pieces):
            f = j * pieces + piece
            columns = slice(piece * features, (piece + 1) * features)
            obuf[slot, 0:2, :, columns] = jnp.dot(
                pre[e, 0:2].reshape(2 * hidden, padded), rbuf[e, f, 0],
                preferred_element_type=jnp.float32,
            ).astype(jnp.bfloat16).reshape(2, hidden, features)
            obuf[slot, 2, :, columns] = jnp.dot(
                pre[e, 2], rbuf[e, f, 1], preferred_element_type=jnp.float32
            ).astype(jnp.bfloat16)
        write(step).start()
        return carry

    lax.fori_loop(0, steps, one, 0)
    for step in range(max(0, steps - slots), steps):
        write(step).wait()


def per_device(tokens, cotangent, routes, gates, expert_weights):
    local, parts, hidden, total_features = expert_weights.shape
    tokens_each, features = tokens.shape
    per_token = routes.shape[1]
    groups = lax.axis_size("expert")
    devices = lax.axis_size("dp")
    chips = devices // CORES
    length = groups * CAP
    meta_rows = -(-2 * per_token // 8) * 8
    padded = -(-length // 128) * 128
    halves = max(1, features // 256)
    count, columns, blocks = chips * halves, features // halves, devices * halves
    sizes = (chips, groups, local, per_token, length)
    any_space = pl.BlockSpec(memory_space=pl.ANY)
    in_vmem = pl.BlockSpec(memory_space=pltpu.VMEM)
    rows, pre = pl.pallas_call(
        functools.partial(exchange_kernel, sizes),
        out_shape=(
            jax.ShapeDtypeStruct((blocks, 2, local, length, columns), jnp.bfloat16),
            jax.ShapeDtypeStruct((local, parts, hidden, padded), jnp.bfloat16),
        ),
        in_specs=[any_space, any_space, in_vmem, in_vmem, any_space],
        out_specs=(any_space, in_vmem),
        scratch_shapes=[
            pltpu.VMEM((CORES, 2, count, groups, tokens_each, columns), jnp.bfloat16),
            pltpu.VMEM((groups, meta_rows, tokens_each), jnp.float32),
            pltpu.VMEM(expert_weights.shape, jnp.bfloat16),
            pltpu.VMEM((local, length, groups * tokens_each), jnp.bfloat16),
            pltpu.VMEM((local * length, 128), jnp.float32),
            pltpu.VMEM((blocks, 2, local, length, columns), jnp.bfloat16),
            pltpu.VMEM((local, parts, hidden, length), jnp.float32),
            pltpu.SemaphoreType.DMA((CORES, 2, count, groups)),
            pltpu.SemaphoreType.DMA((2, count, 2)),
            pltpu.SemaphoreType.DMA((2, count, 2)),
            pltpu.SemaphoreType.DMA((2, count)),
            pltpu.SemaphoreType.DMA,
            pltpu.SemaphoreType.DMA,
            pltpu.SemaphoreType.DMA((groups,)),
            pltpu.SemaphoreType.DMA,
            pltpu.SemaphoreType.DMA((2, halves)),
            pltpu.SemaphoreType.DMA,
            pltpu.SemaphoreType.DMA,
        ],
        compiler_params=pltpu.CompilerParams(
            collective_id=0, has_side_effects=True, vmem_limit_bytes=60 * 1024 * 1024
        ),
        name="exchange",
    )(tokens, cotangent, routes.T, gates.T, expert_weights)
    pieces = max(1, blocks // 4)
    slots = 5
    return pl.pallas_call(
        functools.partial(outer_kernel, pieces, length),
        out_shape=jax.ShapeDtypeStruct(expert_weights.shape, jnp.bfloat16),
        in_specs=[any_space] * 2,
        out_specs=any_space,
        scratch_shapes=[
            pltpu.VMEM((local, parts, hidden, padded), jnp.bfloat16),
            pltpu.VMEM((local, blocks, 2, padded, columns), jnp.bfloat16),
            pltpu.VMEM((slots, parts, hidden, pieces * columns), jnp.bfloat16),
            pltpu.SemaphoreType.DMA((local * (blocks // pieces),)),
            pltpu.SemaphoreType.DMA((slots,)),
            pltpu.SemaphoreType.DMA((local,)),
        ],
        compiler_params=pltpu.CompilerParams(vmem_limit_bytes=60 * 1024 * 1024),
        name="outer",
    )(pre, rows)


def solution(mesh):
    return jax.shard_map(
        per_device,
        mesh=mesh,
        in_specs=(
            P("expert", "dp"),
            P("expert", "dp"),
            P("expert", None),
            P("expert", None),
            P("expert", None, "dp", None),
        ),
        out_specs=P("expert", None, "dp", None),
        check_vma=False,
    )
```
